32 devices in a mesh: gz: 2 (over y), gy: 4 (over z), ta: 4 (over x, core).
Axes of the slice: x: 2, y: 2, z: 4, core: 2. Of those that a mesh axis runs over, the one named last changes fastest.
Arguments:
- movie: float32 [65536, 512], P(('gz', 'gy'), 'ta'), may hold values from 0 to 2
- traces: float32 [2048, 512], P(('gz', 'gy'), 'ta'), may hold values from 0.1 to 2
- entry_comp: int32 [512, 8], P(('gz', 'gy')), may hold values from 0 to 2048, as said below
- footprints: float32 [512, 8, 128], P(('gz', 'gy')), may hold values from 0.05 to 0.5
Outputs:
- traces_out: float32 [2048, 512], P(('gz', 'gy'), 'ta')
- footprints_out: float32 [512, 8, 128], P(('gz', 'gy'))
The draws below stay inside these ranges and needn't reach their ends.
Inputs may be any that keep to these rules, and one draw needn't show every extreme that they name: `entry_comp`: the value 2048 marks an empty slot. In every tile the occupied slots come first; a tile holds up to 8 components, some tile holds 8 in every draw, and a component may appear in several tiles and blocks.
All inputs are finite; a program needn't handle non-finite values.
Results may differ from the reference program's by a relative error of at most 0.0001.
Values sent between devices are 32-bit elements; how exact they have to be, the bound alone decides.
A program may use at most 64 MiB of HBM per device.

```python
import math
import jax
import jax.numpy as jnp
from jax import lax

K = 2048
TILE = 128
SLOTS_T = 8
TILES_DEV = 64
ITERS = 2
NTILES = 512
VOXELS = 65536
FRAMES = 512


def draw_entry_comp(key, part):
    key_level = jax.random.fold_in(key, 11)
    key_count = jax.random.fold_in(key, 12)
    key_full = jax.random.fold_in(key, 13)
    key_comp = jax.random.fold_in(key, 14)
    blocks = NTILES // TILES_DEV
    level = jax.random.randint(key_level, (blocks,), 1, SLOTS_T + 1)
    tile_level = jnp.repeat(level, TILES_DEV, total_repeat_length=NTILES)
    counts = jax.random.randint(key_count, (NTILES,), 0, tile_level + 1)
    full_tile = jax.random.randint(key_full, (), 0, NTILES)
    counts = jnp.where(jnp.arange(NTILES) == full_tile, SLOTS_T, counts)
    comps = jax.random.randint(key_comp, (NTILES, SLOTS_T), 0, K)
    slot = jnp.arange(SLOTS_T)
    return jnp.where(slot[None, :] < counts[:, None], comps, K).astype(jnp.int32)


def block_levels(rng, shape, cuts, least, high):
    def one(axis_at, blocks):
        heights = jax.random.uniform(jax.random.fold_in(jax.random.fold_in(rng, 6), axis_at), (blocks,), jnp.float32, least / len(cuts), high / len(cuts))
        return jnp.repeat(jnp.exp(heights), shape[axis_at] // blocks).reshape((-1,) + (1,) * (len(shape) - axis_at - 1))

    gain = one(*cuts[0])
    for cut in cuts[1:]:
        gain = gain * one(*cut)
    return gain


def setup_inputs(seed: int = 0) -> dict:
    key_of = jax.random.split(jax.random.key(seed), 5)
    movie = jnp.clip(2.0 * jax.random.uniform(key_of[0], (VOXELS, FRAMES), jnp.float32) ** block_levels(key_of[0], (VOXELS, FRAMES), ((0, 8), (1, 4)), -0.2, 0.2), 0.0, 2.0)
    traces = jnp.clip(jnp.exp(math.log(2.0) - 2.9957323 * jax.random.uniform(key_of[1], (K, FRAMES), jnp.float32) ** block_levels(key_of[1], (K, FRAMES), ((0, 8), (1, 4)), -0.2, 0.2)), 0.1, 2.0)
    entry_comp = draw_entry_comp(jax.random.fold_in(key_of[4], 71), 0)
    footprints = jnp.clip(jnp.exp(math.log(0.5) - 2.3025851 * jax.random.uniform(key_of[3], (NTILES, SLOTS_T, TILE), jnp.float32) ** block_levels(key_of[3], (NTILES, SLOTS_T, TILE), ((0, 8),), -0.2, 0.2)), 0.05, 0.5)
    return dict(movie=movie, traces=traces, entry_comp=entry_comp, footprints=footprints)


RIDGE = 1.0


def pick_rows(traces_now, entry_comp):
    padded = jnp.concatenate([traces_now, jnp.zeros((1, traces_now.shape[1]), traces_now.dtype)], 0)
    return jnp.take(padded, entry_comp, axis=0)


def residual_of(tiles, foot, picked):
    recon = jnp.einsum("tjv,tjf->tvf", foot, picked, precision=lax.Precision.HIGHEST)
    return tiles - recon


def reference(movie, traces, entry_comp, footprints):
    ntiles = entry_comp.shape[0]
    frames = movie.shape[1]
    tiles = movie.reshape(ntiles, TILE, frames)
    valid = (entry_comp < K).astype(footprints.dtype)
    foot = footprints * valid[:, :, None]
    flat = entry_comp.reshape(-1)
    traces_now = traces
    for step in range(ITERS):
        picked = pick_rows(traces_now, entry_comp)
        resid = residual_of(tiles, foot, picked)
        cover = jnp.sum(foot, axis=1)
        proj = jnp.einsum("tjv,tvf->tjf", foot, resid, precision=lax.Precision.HIGHEST)
        curv = jnp.einsum("tjv,tv->tj", foot, cover, precision=lax.Precision.HIGHEST)
        numer = jax.ops.segment_sum(proj.reshape(-1, frames), flat, K + 1)[:K]
        denom = jax.ops.segment_sum(curv.reshape(-1), flat, K + 1)[:K]
        traces_now = jnp.maximum(traces_now + numer / (denom + RIDGE)[:, None], 0.0)
        picked = pick_rows(traces_now, entry_comp)
        resid = residual_of(tiles, foot, picked)
        grad = jnp.einsum("tvf,tjf->tjv", resid, picked, precision=lax.Precision.HIGHEST)
        gram = jnp.einsum("tjf,tif->tji", picked, picked, precision=lax.Precision.HIGHEST)
        dsp = jnp.sum(gram, axis=2) + RIDGE
        foot = jnp.maximum(foot + grad / dsp[:, :, None], 0.0) * valid[:, :, None]
    return traces_now, foot
```

```python
import functools

import jax
import jax.numpy as jnp
from jax import lax
from jax.experimental import pallas as pl
from jax.experimental.pallas import tpu as pltpu
from jax.sharding import PartitionSpec as P

ITERS = 2
RIDGE = 1.0
LANES = 128
MESH = pl.DeviceIdType.MESH
F32 = jnp.float32
BF16 = jnp.bfloat16
NT = (((1,), (1,)), ((), ()))
NN = (((1,), (0,)), ((), ()))


def split(x):
    hi = x.astype(BF16)
    return hi, (x - hi.astype(F32)).astype(BF16)


def dot(a, b, dims=NN):
    return lax.dot_general(a, b, dims, preferred_element_type=F32)


def exact(a, b, dims=NN):
    return lax.dot_general(a, b, dims, precision=lax.Precision.HIGHEST, preferred_element_type=F32)


def column(row):
    n = row.shape[1]
    r = lax.broadcasted_iota(jnp.int32, (n, n), 0)
    c = lax.broadcasted_iota(jnp.int32, (n, n), 1)
    return jnp.sum(jnp.where(r == c, jnp.broadcast_to(row, (n, n)), 0.0), axis=1, keepdims=True)


def kernel(
    G, Y, T, slots,
    movie_hbm, traces, comp, foot_in, tr_out, foot_out,
    mv, m2, mt, oh, oht, call, valid, foot, picked, own,
    half, curv, crow, proj, xs, nsend, nrecv, dsend, drecv, psend, precv,
    grad, dsp, grecv, dspr, gsum, dsps, grecv2, dspr2,
    load_sem, c_s, c_r, half_s, half_r, curv_s, curv_r, proj_s, proj_r,
    num_s, num_r, den_s, den_r, pick_s, pick_r, g1_s, g1_r, d1_s, d1_r, g2_s, g2_r, d2_s, d2_r, f_s, f_r,
):
    gz, gy, ta = lax.axis_index("gz"), lax.axis_index("gy"), lax.axis_index("ta")
    S, V = foot_in.shape
    R, F = traces.shape
    H = Y * R
    K = G * H
    NG = S // LANES
    TG = LANES // slots
    hb = S // 2
    hg = NG // 2
    pairs = T // 2
    core = lax.rem(ta, 2)
    pair = lax.div(ta, 2)
    mate = ta + 1 - 2 * core

    load = pltpu.make_async_copy(movie_hbm, mv, load_sem)
    load.start()

    def zpeer(d):
        return {"gz": lax.rem(gz + d, G)}

    def ypeer(d):
        return {"gy": lax.rem(gy + d, Y)}

    def tpeer(d):
        return {"ta": lax.rem(pair + d, pairs) * 2 + core}

    targets = [zpeer(d) for d in range(1, G)] + [ypeer(d) for d in range(1, Y)]
    targets += [tpeer(d) for d in range(1, pairs)] + [{"ta": mate}]
    barrier = pltpu.get_barrier_semaphore()
    for target in targets:
        pl.semaphore_signal(barrier, inc=1, device_id=target, device_id_type=MESH)
    pl.semaphore_wait(barrier, len(targets))

    sent = []

    def send(src, dst, ssem, rsem, target):
        copy = pltpu.make_async_remote_copy(
            src_ref=src, dst_ref=dst, send_sem=ssem, recv_sem=rsem, device_id=target, device_id_type=MESH
        )
        copy.start()
        sent.append(copy)
        return copy

    mine = pl.ds(pl.multiple_of(gy * R, R), R)

    def gather_half(step):
        return [
            send(own.at[step], half.at[step, mine], half_s.at[step, d], half_r.at[step, d], ypeer(d))
            for d in range(1, Y)
        ]

    own[0] = traces[...]
    waits_half = gather_half(0)
    call[0] = comp[...]
    waits_c = [send(call.at[0], call.at[d], c_s.at[d], c_r.at[d], zpeer(d)) for d in range(1, G)]

    for g in range(NG):
        rows = pl.ds(g * LANES, LANES)
        ok = (column(comp[g][0:1, :]) < float(K)).astype(F32)
        okb = jnp.broadcast_to(ok, (LANES, V))
        valid[rows, :] = okb
        foot[0, rows, :] = foot_in[rows, :] * okb

    load.wait()

    def split_tile(t, _):
        m = mv[pl.ds(pl.multiple_of(t * V, V), V), :]
        at = pl.ds(pl.multiple_of(t * V, V), V)
        hi, lo = split(m)
        m2[at, 0:F] = hi
        m2[at, F : 2 * F] = lo
        at = pl.ds(pl.multiple_of(t * F, F), F)
        hi, lo = split(m.T)
        mt[at, 0:V] = hi
        mt[at, V : 2 * V] = lo
        return _

    lax.fori_loop(0, NG * TG, split_tile, 0)

    blk_r = lax.broadcasted_iota(jnp.int32, (LANES, LANES), 0) // slots
    blk_c = lax.broadcasted_iota(jnp.int32, (LANES, LANES), 1) // slots
    same = blk_r == blk_c

    def tiles_dot(big, depth, g, rows):
        hi, lo = split(rows)
        w = jnp.concatenate(
            [jnp.concatenate([hi, hi], axis=1), jnp.concatenate([lo, lo], axis=1)], axis=0
        )
        at = pl.ds(pl.multiple_of(g * (TG * depth), TG * depth), TG * depth)
        res = dot(big[at, :], w, NT)
        res = res[:, 0:LANES] + res[:, LANES : 2 * LANES]
        acc = jnp.zeros((depth, LANES), F32)
        lane = lax.broadcasted_iota(jnp.int32, (depth, LANES), 1) // slots
        for t in range(TG):
            acc = jnp.where(lane == t, res[t * depth : (t + 1) * depth, :], acc)
        return acc.T

    def footgram(step, g):
        rows = pl.ds(pl.multiple_of(g * LANES, LANES), LANES)
        f = foot[step, rows, :]
        return jnp.where(same, exact(f, f, NT), 0.0)

    def curvature(step):
        def one(g, _):
            gram = footgram(step, g)
            curv[step, 0, g] = jnp.broadcast_to(jnp.sum(gram, axis=0, keepdims=True), (8, LANES))
            return _

        lax.fori_loop(0, NG, one, 0)
        return [
            send(curv.at[step, 0], curv.at[step, d], curv_s.at[step, d], curv_r.at[step, d], zpeer(d))
            for d in range(1, G)
        ]

    waits_curv = curvature(0)

    for w in waits_c:
        w.wait_recv()
    base = gz * H
    for d in range(G):
        for g in range(NG):
            row = call[d, g][0:1, :]
            cols = pl.ds((d * NG + g) * LANES, LANES)
            ids = (lax.broadcasted_iota(jnp.int32, (H, LANES), 0) + base).astype(F32)
            oht[:, cols] = jnp.where(ids == row, 1.0, 0.0).astype(BF16)
            ids = (lax.broadcasted_iota(jnp.int32, (LANES, H), 1) + base).astype(F32)
            oh[cols, :] = jnp.where(ids == column(row), 1.0, 0.0).astype(BF16)

    def pick(step, waits):
        half[step, mine, :] = own[step]
        for w in waits:
            w.wait_recv()
        hi, lo = split(half[step])
        both = jnp.concatenate([hi, lo], axis=1)
        out = []
        for d in list(range(1, G)) + [0]:
            res = dot(oh[pl.ds(d * S, S), :], both)
            res = res[:, 0:F] + res[:, F : 2 * F]
            if d:
                psend[step, d - 1] = res
                out.append(
                    send(
                        psend.at[step, d - 1], precv.at[step, d - 1],
                        pick_s.at[step, d], pick_r.at[step, d], zpeer(G - d),
                    )
                )
            else:
                total = res
        for d in range(1, G):
            out[d - 1].wait_recv()
            total = total + precv[step, d - 1]
        picked[...] = total

    pick(0, waits_half)

    for it in range(ITERS):
        def project(g, _, it=it):
            rows = pl.ds(pl.multiple_of(g * LANES, LANES), LANES)
            p = tiles_dot(mt, F, g, foot[it, rows, :])
            proj[it, 0, rows, :] = p - exact(footgram(it, g), picked[rows, :])
            return _

        lax.fori_loop(0, NG, project, 0)
        waits = [
            send(proj.at[it, 0], proj.at[it, d], proj_s.at[it, d], proj_r.at[it, d], zpeer(d))
            for d in range(1, G)
        ]
        for w in waits_curv:
            w.wait_recv()
        for d in range(G):
            for g in range(NG):
                hi, lo = split(curv[it, d, g])
                crow[:, (d * NG + g) * LANES : (d * NG + g + 1) * LANES] = jnp.concatenate([hi, lo], axis=0)
        for d in range(G):
            if d:
                waits[d - 1].wait_recv()
            hi, lo = split(proj[it, d])
            xs[pl.ds(d * S, S), 0:F] = hi
            xs[pl.ds(d * S, S), F : 2 * F] = lo
        waits = []
        for d in list(range(1, Y)) + [0]:
            to = lax.rem(gy + d, Y)
            block = oht[pl.ds(pl.multiple_of(to * R, R), R), :]
            num = dot(block, xs[...])
            num = num[:, 0:F] + num[:, F : 2 * F]
            den = dot(crow[...], block, NT)
            den = den[0:8] + den[8:16]
            if d:
                nsend[it, d - 1] = num
                dsend[it, d - 1] = den
                waits.append(
                    send(nsend.at[it, d - 1], nrecv.at[it, d - 1], num_s.at[it, d], num_r.at[it, d], ypeer(d))
                )
                waits.append(
                    send(dsend.at[it, d - 1], drecv.at[it, d - 1], den_s.at[it, d], den_r.at[it, d], ypeer(d))
                )
        for w in waits:
            w.wait_recv()
        for d in range(1, Y):
            num = num + nrecv[it, d - 1]
            den = den + drecv[it, d - 1]
        own[it + 1] = jnp.maximum(own[it] + num / (column(den[0:1, :]) + RIDGE), 0.0)
        pick(it + 1, gather_half(it + 1))

        def gradient(g, _, it=it):
            rows = pl.ds(pl.multiple_of(g * LANES, LANES), LANES)
            p = picked[rows, :]
            gram = jnp.where(same, exact(p, p, NT), 0.0)
            grad[it, rows, :] = tiles_dot(m2, V, g, p) - exact(gram, foot[it, rows, :])
            dsp[it, g] = jnp.broadcast_to(jnp.sum(gram, axis=0, keepdims=True), (8, LANES))
            return _

        lax.fori_loop(0, NG, gradient, 0)
        keep = pl.ds(pl.multiple_of(core * hb, hb), hb)
        give = pl.ds(pl.multiple_of((1 - core) * hb, hb), hb)
        a = send(grad.at[it, give], grecv.at[it], g1_s.at[it], g1_r.at[it], {"ta": mate})
        b = send(dsp.at[it, pl.ds((1 - core) * hg, hg)], dspr.at[it], d1_s.at[it], d1_r.at[it], {"ta": mate})
        a.wait_recv()
        b.wait_recv()
        gsum[it] = grad[it, keep, :] + grecv[it]
        dsps[it] = dsp[it, pl.ds(core * hg, hg)] + dspr[it]
        waits = []
        for d in range(1, pairs):
            waits.append(send(gsum.at[it], grecv2.at[it, d - 1], g2_s.at[it, d], g2_r.at[it, d], tpeer(d)))
            waits.append(send(dsps.at[it], dspr2.at[it, d - 1], d2_s.at[it, d], d2_r.at[it, d], tpeer(d)))
        for w in waits:
            w.wait_recv()
        gt, dt = gsum[it], dsps[it]
        for d in range(1, pairs):
            gt = gt + grecv2[it, d - 1]
            dt = dt + dspr2[it, d - 1]
        step = jnp.concatenate([column(dt[g][0:1, :]) for g in range(hg)], axis=0) + RIDGE
        foot[it + 1, keep, :] = jnp.maximum(foot[it, keep, :] + gt / step, 0.0) * valid[keep, :]
        a = send(foot.at[it + 1, keep], foot.at[it + 1, keep], f_s.at[it], f_r.at[it], {"ta": mate})
        if it == ITERS - 1:
            tr_out[...] = own[ITERS]
        a.wait_recv()
        if it < ITERS - 1:
            waits_curv = curvature(it + 1)
    foot_out[...] = foot[ITERS]
    for copy in sent:
        copy.wait_send()


def solution(mesh):
    G, Y, T = (mesh.shape[a] for a in ("gz", "gy", "ta"))

    def local(movie, traces, entry_comp, footprints):
        tiles, slots = entry_comp.shape
        V = footprints.shape[2]
        R, F = traces.shape
        S, H = tiles * slots, Y * R
        NG = S // LANES
        hb, hg, pairs = S // 2, NG // 2, T // 2
        comp = jnp.broadcast_to(entry_comp.astype(F32).reshape(NG, 1, LANES), (NG, 8, LANES))
        vm = pltpu.VMEM
        dma = pltpu.SemaphoreType.DMA
        I = ITERS
        np_ = max(pairs - 1, 1)
        scratch = [
            vm(movie.shape, F32), vm((tiles * V, 2 * F), BF16), vm((tiles * F, 2 * V), BF16),
            vm((G * S, H), BF16), vm((H, G * S), BF16), vm((G, NG, 8, LANES), F32),
            vm((S, V), F32), vm((I + 1, S, V), F32), vm((S, F), F32), vm((I + 1, R, F), F32),
            vm((I + 1, H, F), F32), vm((I, G, NG, 8, LANES), F32), vm((16, G * S), BF16),
            vm((I, G, S, F), F32), vm((G * S, 2 * F), BF16),
            vm((I, Y - 1, R, F), F32), vm((I, Y - 1, R, F), F32),
            vm((I, Y - 1, 8, R), F32), vm((I, Y - 1, 8, R), F32),
            vm((I + 1, G - 1, S, F), F32), vm((I + 1, G - 1, S, F), F32),
            vm((I, S, V), F32), vm((I, NG, 8, LANES), F32),
            vm((I, hb, V), F32), vm((I, hg, 8, LANES), F32), vm((I, hb, V), F32), vm((I, hg, 8, LANES), F32),
            vm((I, np_, hb, V), F32), vm((I, np_, hg, 8, LANES), F32),
            dma, dma((G,)), dma((G,)), dma((I + 1, Y)), dma((I + 1, Y)), dma((I, G)), dma((I, G)),
            dma((I, G)), dma((I, G)), dma((I, Y)), dma((I, Y)), dma((I, Y)), dma((I, Y)),
            dma((I + 1, G)), dma((I + 1, G)), dma((I,)), dma((I,)), dma((I,)), dma((I,)),
            dma((I, pairs)), dma((I, pairs)), dma((I, pairs)), dma((I, pairs)), dma((I,)), dma((I,)),
        ]
        vs = pl.BlockSpec(memory_space=pltpu.VMEM)
        tr, ft = pl.pallas_call(
            functools.partial(kernel, G, Y, T, slots),
            out_shape=(jax.ShapeDtypeStruct((R, F), F32), jax.ShapeDtypeStruct((S, V), F32)),
            in_specs=[pl.BlockSpec(memory_space=pl.ANY), vs, vs, vs],
            out_specs=(vs, vs),
            scratch_shapes=scratch,
            compiler_params=pltpu.CompilerParams(
                collective_id=0, has_side_effects=True, vmem_limit_bytes=56 * 1024 * 1024
            ),
        )(movie, traces, comp, footprints.reshape(S, V))
        return tr, ft.reshape(tiles, slots, V)

    placed = (
        P(("gz", "gy"), "ta"),
        P(("gz", "gy"), "ta"),
        P(("gz", "gy"), None),
        P(("gz", "gy"), None, None),
    )
    return jax.shard_map(
        local,
        mesh=mesh,
        in_specs=placed,
        out_specs=(P(("gz", "gy"), "ta"), P(("gz", "gy"), None, None)),
        check_vma=False,
    )
```

```python
import functools

import jax
import jax.numpy as jnp
from jax import lax
from jax.experimental import pallas as pl
from jax.experimental.pallas import tpu as pltpu
from jax.sharding import PartitionSpec as P

ITERS = 2
RIDGE = 1.0
LANES = 128
MESH = pl.DeviceIdType.MESH
F32 = jnp.float32
BF16 = jnp.bfloat16
NT = (((1,), (1,)), ((), ()))
NN = (((1,), (0,)), ((), ()))


def split(x):
    hi = x.astype(BF16)
    return hi, (x - hi.astype(F32)).astype(BF16)


def dot(a, b, dims=NN):
    return lax.dot_general(a, b, dims, preferred_element_type=F32)


def exact(a, b, dims=NN):
    return lax.dot_general(a, b, dims, precision=lax.Precision.HIGHEST, preferred_element_type=F32)


def column(row):
    n = row.shape[1]
    r = lax.broadcasted_iota(jnp.int32, (n, n), 0)
    c = lax.broadcasted_iota(jnp.int32, (n, n), 1)
    return jnp.sum(jnp.where(r == c, jnp.broadcast_to(row, (n, n)), 0.0), axis=1, keepdims=True)


def kernel(
    G, Y, T, slots,
    movie_hbm, traces, comp, foot_in, tr_out, foot_out,
    mv, m2, mt, oh, oht, oha, call, valid, foot, picked, own,
    full, curv, crow, xs, ysend, yrecv, acc, crecv,
    grad, dsp, grecv, dspr, gsum, dsps, grecv2, dspr2,
    load_sem, c_s, c_r, ch_s, ch_r, fy_s, fy_r, curv_s, curv_r,
    y_s, y_r, k_s, k_r, g1_s, g1_r, d1_s, d1_r, g2_s, g2_r, d2_s, d2_r, f_s, f_r,
):
    gz, gy, ta = lax.axis_index("gz"), lax.axis_index("gy"), lax.axis_index("ta")
    S, V = foot_in.shape
    R, F = traces.shape
    H = Y * R
    K = G * H
    NG = S // LANES
    TG = LANES // slots
    hb = S // 2
    hg = NG // 2
    pairs = T // 2
    core = lax.rem(ta, 2)
    pair = lax.div(ta, 2)
    mate = ta + 1 - 2 * core

    load = pltpu.make_async_copy(movie_hbm, mv, load_sem)
    load.start()

    def zpeer(d):
        return {"gz": lax.rem(gz + d, G)}

    def tpeer(d):
        return {"ta": lax.rem(pair + d, pairs) * 2 + core}

    others = [(d, e) for d in range(G) for e in range(Y) if d or e]

    def peer(d, e):
        return {"gz": lax.rem(gz + d, G), "gy": lax.rem(gy + e, Y)}

    targets = [peer(d, e) for d, e in others]
    targets += [tpeer(d) for d in range(1, pairs)] + [{"ta": mate}]
    barrier = pltpu.get_barrier_semaphore()
    for target in targets:
        pl.semaphore_signal(barrier, inc=1, device_id=target, device_id_type=MESH)
    pl.semaphore_wait(barrier, len(targets))

    ends = []

    def send(src, dst, ssem, rsem, target):
        copy = pltpu.make_async_remote_copy(
            src_ref=src, dst_ref=dst, send_sem=ssem, recv_sem=rsem, device_id=target, device_id_type=MESH
        )
        copy.start()
        ends.append(copy)
        return copy

    def landed(ref, sem):
        pltpu.make_async_remote_copy(
            src_ref=ref, dst_ref=ref, send_sem=sem, recv_sem=sem, device_id={"ta": mate}, device_id_type=MESH
        ).wait_recv()

    def descriptor(src, dst, ssem, rsem, target):
        return pltpu.make_async_remote_copy(
            src_ref=src, dst_ref=dst, send_sem=ssem, recv_sem=rsem, device_id=target, device_id_type=MESH
        )

    def along(step, way, b):
        ref = full.at[step, 0, b]
        return descriptor(ref, ref, ch_s.at[step, way, b], ch_r.at[step, way, b], {"gy": gy + 1 - 2 * way})

    def across(step, b):
        return [
            descriptor(full.at[step, 0, b], full.at[step, d, b], fy_s.at[step, d, b], fy_r.at[step, d, b], zpeer(d))
            for d in range(1, G)
        ]

    def more(way):
        return gy < Y - 1 if way == 0 else gy > 0

    def block_of(way, s):
        return gy - s if way == 0 else gy + s

    def inside(b):
        return jnp.logical_and(b >= 0, b < Y)

    def gather_start(step):
        full[step, 0, gy] = own[step]
        for way in (0, 1):
            pl.when(more(way))(lambda way=way: along(step, way, gy).start())
        for c in across(step, gy):
            c.start()

    def gather_stage(step, s):
        for way in (0, 1):
            b = block_of(way, s + 1)

            @pl.when(inside(b))
            def _(way=way, b=b):
                landed(full.at[step, 0, b], ch_r.at[step, way, b])
                pl.when(more(way))(lambda: along(step, way, b).start())
                for c in across(step, b):
                    c.start()

    def gather_end(step):
        for s in range(Y):
            for way in (0, 1):
                b = block_of(way, s)

                @pl.when(jnp.logical_and(inside(b), more(way)))
                def _(way=way, b=b):
                    along(step, way, b).wait_send()

        for b in range(Y):
            for c in across(step, b):
                c.wait_send()

    own[0] = traces[...]
    gather_start(0)
    call[0, 0] = comp[...]
    waits_c = [
        send(call.at[0, 0], call.at[d, e], c_s.at[d, e], c_r.at[d, e], peer(d, e)) for d, e in others
    ]

    for g in range(NG):
        rows = pl.ds(g * LANES, LANES)
        ok = (column(comp[g : g + 1, :]) < float(K)).astype(F32)
        okb = jnp.broadcast_to(ok, (LANES, V))
        valid[rows, :] = okb
        foot[0, rows, :] = foot_in[rows, :] * okb

    def split_tile(t, _):
        m = mv[pl.ds(pl.multiple_of(t * V, V), V), :]
        at = pl.ds(pl.multiple_of(t * V, V), V)
        hi, lo = split(m)
        m2[at, 0:F] = hi
        m2[at, F : 2 * F] = lo
        at = pl.ds(pl.multiple_of(t * F, F), F)
        hi, lo = split(m.T)
        mt[at, 0:V] = hi
        mt[at, V : 2 * V] = lo
        return _

    blk_r = lax.broadcasted_iota(jnp.int32, (LANES, LANES), 0) // slots
    blk_c = lax.broadcasted_iota(jnp.int32, (LANES, LANES), 1) // slots
    same = blk_r == blk_c

    def tiles_dot(big, depth, g, rows):
        hi, lo = split(rows)
        w = jnp.concatenate(
            [jnp.concatenate([hi, hi], axis=1), jnp.concatenate([lo, lo], axis=1)], axis=0
        )
        at = pl.ds(pl.multiple_of(g * (TG * depth), TG * depth), TG * depth)
        res = dot(big[at, :], w, NT)
        res = res[:, 0:LANES] + res[:, LANES : 2 * LANES]
        out = jnp.zeros((depth, LANES), F32)
        lane = lax.broadcasted_iota(jnp.int32, (depth, LANES), 1) // slots
        for t in range(TG):
            out = jnp.where(lane == t, res[t * depth : (t + 1) * depth, :], out)
        return out.T

    def footgram(step, g):
        rows = pl.ds(pl.multiple_of(g * LANES, LANES), LANES)
        f = foot[step, rows, :]
        return jnp.where(same, exact(f, f, NT), 0.0)

    def curvature(step):
        curv[step, 0, 0] = jnp.zeros_like(curv[step, 0, 0])
        for g in range(NG):
            curv[step, 0, 0, g : g + 1, :] = jnp.sum(footgram(step, g), axis=0, keepdims=True)
        return [
            send(curv.at[step, 0, 0], curv.at[step, d, e], curv_s.at[step, d, e], curv_r.at[step, d, e], peer(d, e))
            for d, e in others
        ]

    waits_curv = curvature(0)
    load.wait()
    tiles = NG * TG
    cuts = [tiles * i // Y for i in range(Y + 1)]
    for s in range(Y - 1):
        lax.fori_loop(cuts[s], cuts[s + 1], split_tile, 0)
        gather_stage(0, s)
    lax.fori_loop(cuts[Y - 1], cuts[Y], split_tile, 0)

    for g in range(NG):
        row = call[0, 0, g : g + 1, :]
        cols = pl.ds(g * LANES, LANES)
        ids = lax.broadcasted_iota(jnp.int32, (K, LANES), 0).astype(F32)
        oht[:, cols] = jnp.where(ids == row, 1.0, 0.0).astype(BF16)
        col = column(row)
        for d in range(G):
            ids = lax.broadcasted_iota(jnp.int32, (LANES, H), 1) + lax.rem(gz + G - d, G) * H
            oh[d, cols, :] = jnp.where(ids.astype(F32) == col, 1.0, 0.0).astype(BF16)

    def pick(step):
        total = jnp.zeros((S, F), F32)
        for d in range(G):
            if d:
                for b in range(Y):
                    landed(full.at[step, d, b], fy_r.at[step, d, b])
            hi, lo = split(full[step, d].reshape(H, F))
            res = dot(oh[d], jnp.concatenate([hi, lo], axis=1))
            total = total + res[:, 0:F] + res[:, F : 2 * F]
        picked[...] = total

    pick(0)
    for w in waits_c:
        w.wait_recv()
    first = (gz * Y + gy) * R
    every = [(0, 0)] + others
    for n, (d, e) in enumerate(every):
        for g in range(NG):
            ids = (lax.broadcasted_iota(jnp.int32, (R, LANES), 0) + first).astype(F32)
            hit = jnp.where(ids == call[d, e, g : g + 1, :], 1.0, 0.0)
            oha[:, pl.ds((n * NG + g) * LANES, LANES)] = hit.astype(BF16)

    upper = lax.div(2 * gy, Y)

    def order(i):
        down = Y - 1 - i - lax.div(gy + 1 + i, Y)
        up = i + lax.div(Y + i - gy, Y)
        return (1 - upper) * down + upper * up

    for it in range(ITERS):
        def project(g, _, it=it):
            rows = pl.ds(pl.multiple_of(g * LANES, LANES), LANES)
            p = tiles_dot(mt, F, g, foot[it, rows, :]) - exact(footgram(it, g), picked[rows, :])
            hi, lo = split(p)
            xs[rows, 0:F] = hi
            xs[rows, F : 2 * F] = lo
            return _

        lax.fori_loop(0, NG, project, 0)

        def partial(z, b):
            at = pl.ds(pl.multiple_of((z * Y + b) * R, R), R)
            num = dot(oht[at, :], xs[...])
            return num[:, 0:F] + num[:, F : 2 * F]

        blocks = [order(i) for i in range(Y - 1)] + [gy]
        for b in blocks:
            for d in range(1, G):
                ysend[it, d - 1, b] = partial(lax.rem(gz + d, G), b)
                send(ysend.at[it, d - 1, b], yrecv.at[it, d - 1, b], y_s.at[it, d, b], y_r.at[it, d, b], zpeer(d))
            acc[it, b] = partial(gz, b)

        def pass_on(b, it=it):
            up = lax.div(Y + b - gy - 1, Y)
            way = 1 - up
            came = gy + 1 - 2 * up
            total = acc[it, b]
            for d in range(1, G):
                landed(yrecv.at[it, d - 1, b], y_r.at[it, d, b])
                total = total + yrecv[it, d - 1, b]
            acc[it, b] = total

            @pl.when(inside(came))
            def _():
                landed(crecv.at[it, way, b], k_r.at[it, way, b])
                acc[it, b] = acc[it, b] + crecv[it, way, b]

            send(acc.at[it, b], crecv.at[it, way, b], k_s.at[it, b], k_r.at[it, way, b], {"gy": gy + 2 * up - 1})

        for b in blocks[: Y - 1]:
            pass_on(b)

        for w in waits_curv:
            w.wait_recv()
        for n, (d, e) in enumerate(every):
            for g in range(NG):
                hi, lo = split(jnp.broadcast_to(curv[it, d, e, g : g + 1, :], (8, LANES)))
                crow[:, (n * NG + g) * LANES : (n * NG + g + 1) * LANES] = jnp.concatenate([hi, lo], axis=0)
        den = dot(crow[...], oha[...], NT)
        den = column(den[0:1] + den[8:9]) + RIDGE

        for d in range(1, G):
            landed(yrecv.at[it, d - 1, gy], y_r.at[it, d, gy])
            acc[it, gy] = acc[it, gy] + yrecv[it, d - 1, gy]
        for way in (0, 1):

            @pl.when(more(1 - way))
            def _(way=way, it=it):
                landed(crecv.at[it, way, gy], k_r.at[it, way, gy])
                acc[it, gy] = acc[it, gy] + crecv[it, way, gy]

        own[it + 1] = jnp.maximum(own[it] + acc[it, gy] / den, 0.0)
        gather_start(it + 1)
        for s in range(Y - 1):
            gather_stage(it + 1, s)
        pick(it + 1)

        def gradient(g, _, it=it):
            rows = pl.ds(pl.multiple_of(g * LANES, LANES), LANES)
            p = picked[rows, :]
            gram = jnp.where(same, exact(p, p, NT), 0.0)
            grad[it, rows, :] = tiles_dot(m2, V, g, p) - exact(gram, foot[it, rows, :])
            dsp[it, g] = jnp.broadcast_to(jnp.sum(gram, axis=0, keepdims=True), (8, LANES))
            return _

        lax.fori_loop(0, NG, gradient, 0)
        keep = pl.ds(pl.multiple_of(core * hb, hb), hb)
        give = pl.ds(pl.multiple_of((1 - core) * hb, hb), hb)
        a = send(grad.at[it, give], grecv.at[it], g1_s.at[it], g1_r.at[it], {"ta": mate})
        b = send(dsp.at[it, pl.ds((1 - core) * hg, hg)], dspr.at[it], d1_s.at[it], d1_r.at[it], {"ta": mate})
        a.wait_recv()
        b.wait_recv()
        gsum[it] = grad[it, keep, :] + grecv[it]
        dsps[it] = dsp[it, pl.ds(core * hg, hg)] + dspr[it]
        waits = []
        for d in range(1, pairs):
            waits.append(send(gsum.at[it], grecv2.at[it, d - 1], g2_s.at[it, d], g2_r.at[it, d], tpeer(d)))
            waits.append(send(dsps.at[it], dspr2.at[it, d - 1], d2_s.at[it, d], d2_r.at[it, d], tpeer(d)))
        for w in waits:
            w.wait_recv()
        gt, dt = gsum[it], dsps[it]
        for d in range(1, pairs):
            gt = gt + grecv2[it, d - 1]
            dt = dt + dspr2[it, d - 1]
        step = jnp.concatenate([column(dt[g][0:1, :]) for g in range(hg)], axis=0) + RIDGE
        foot[it + 1, keep, :] = jnp.maximum(foot[it, keep, :] + gt / step, 0.0) * valid[keep, :]
        a = send(foot.at[it + 1, keep], foot.at[it + 1, keep], f_s.at[it], f_r.at[it], {"ta": mate})
        if it == ITERS - 1:
            tr_out[...] = own[ITERS]
        a.wait_recv()
        if it < ITERS - 1:
            waits_curv = curvature(it + 1)
    foot_out[...] = foot[ITERS]
    for step in range(ITERS + 1):
        gather_end(step)
    for copy in ends:
        copy.wait_send()


def solution(mesh):
    G, Y, T = (mesh.shape[a] for a in ("gz", "gy", "ta"))

    def local(movie, traces, entry_comp, footprints):
        tiles, slots = entry_comp.shape
        V = footprints.shape[2]
        R, F = traces.shape
        S, H = tiles * slots, Y * R
        NG = S // LANES
        hb, hg, pairs = S // 2, NG // 2, T // 2
        NP = -(-NG // 8) * 8
        comp = jnp.pad(entry_comp.astype(F32).reshape(NG, LANES), ((0, NP - NG), (0, 0)))
        vm = pltpu.VMEM
        dma = pltpu.SemaphoreType.DMA
        I = ITERS
        np_ = max(pairs - 1, 1)
        scratch = [
            vm(movie.shape, F32), vm((tiles * V, 2 * F), BF16), vm((tiles * F, 2 * V), BF16),
            vm((G, S, H), BF16), vm((G * H, S), BF16), vm((R, G * Y * S), BF16), vm((G, Y, NP, LANES), F32),
            vm((S, V), F32), vm((I + 1, S, V), F32), vm((S, F), F32), vm((I + 1, R, F), F32),
            vm((I + 1, G, Y, R, F), F32), vm((I, G, Y, NP, LANES), F32), vm((16, G * Y * S), BF16),
            vm((S, 2 * F), BF16), vm((I, G - 1, Y, R, F), F32), vm((I, G - 1, Y, R, F), F32),
            vm((I, Y, R, F), F32), vm((I, 2, Y, R, F), F32),
            vm((I, S, V), F32), vm((I, NG, 8, LANES), F32),
            vm((I, hb, V), F32), vm((I, hg, 8, LANES), F32), vm((I, hb, V), F32), vm((I, hg, 8, LANES), F32),
            vm((I, np_, hb, V), F32), vm((I, np_, hg, 8, LANES), F32),
            dma, dma((G, Y)), dma((G, Y)), dma((I + 1, 2, Y)), dma((I + 1, 2, Y)),
            dma((I + 1, G, Y)), dma((I + 1, G, Y)), dma((I, G, Y)), dma((I, G, Y)),
            dma((I, G, Y)), dma((I, G, Y)), dma((I, Y)), dma((I, 2, Y)),
            dma((I,)), dma((I,)), dma((I,)), dma((I,)),
            dma((I, pairs)), dma((I, pairs)), dma((I, pairs)), dma((I, pairs)), dma((I,)), dma((I,)),
        ]
        vs = pl.BlockSpec(memory_space=pltpu.VMEM)
        tr, ft = pl.pallas_call(
            functools.partial(kernel, G, Y, T, slots),
            out_shape=(jax.ShapeDtypeStruct((R, F), F32), jax.ShapeDtypeStruct((S, V), F32)),
            in_specs=[pl.BlockSpec(memory_space=pl.ANY), vs, vs, vs],
            out_specs=(vs, vs),
            scratch_shapes=scratch,
            compiler_params=pltpu.CompilerParams(
                collective_id=0, has_side_effects=True, vmem_limit_bytes=56 * 1024 * 1024
            ),
        )(movie, traces, comp, footprints.reshape(S, V))
        return tr, ft.reshape(tiles, slots, V)

    placed = (
        P(("gz", "gy"), "ta"),
        P(("gz", "gy"), "ta"),
        P(("gz", "gy"), None),
        P(("gz", "gy"), None, None),
    )
    return jax.shard_map(
        local,
        mesh=mesh,
        in_specs=placed,
        out_specs=(P(("gz", "gy"), "ta"), P(("gz", "gy"), None, None)),
        check_vma=False,
    )
```
